256 devices in a mesh: pipe: 4 (over y_hi, core), expert: 64 (over x, z, y_lo).
Axes of the slice: x: 4, y: 4 (y_hi: 2, y_lo: 2; y = y_hi * 2 + y_lo), z: 8, core: 2. Of those that a mesh axis runs over, the one named last changes fastest.
Arguments:
- forward_input: bfloat16 [4, 8192, 3584], P('pipe', 'expert'), may hold values from -6 to 6
- forward_route: int32 [4, 8192, 1], P('pipe', 'expert'), may hold values from 0 to 15; in each aligned block of 128 rows (0 to 127, 128 to 255, ..., all dimensions but the last counted through in order) at most 12 rows name the same one
- forward_weight: float32 [4, 8192, 1], P('pipe', 'expert'), may hold values from 0.3 to 3
- backward_input: bfloat16 [4, 8192, 3584], P('pipe', 'expert'), may hold values from -6 to 6
- backward_route: int32 [4, 8192, 1], P('pipe', 'expert'), may hold values from 0 to 15; in each aligned block of 128 rows (0 to 127, 128 to 255, ..., all dimensions but the last counted through in order) at most 12 rows name the same one
- backward_weight: float32 [4, 8192, 1], P('pipe', 'expert'), may hold values from 0.3 to 3
- output_grad: bfloat16 [4, 8192, 3584], P('pipe', 'expert'), may hold values from -6 to 6
- norm_gain: float32 [4, 3584], P('pipe'), may hold values from 0.1 to 1.9
- gate_weight: bfloat16 [4, 3584, 16384], P('pipe', None, 'expert'), may hold values from -0.09375 to 0.09375
- up_weight: bfloat16 [4, 3584, 16384], P('pipe', None, 'expert'), may hold values from -0.09375 to 0.09375
- down_weight: bfloat16 [4, 16384, 3584], P('pipe', 'expert'), may hold values from -0.1875 to 0.1875
Outputs:
- next_input: bfloat16 [4, 8192, 3584], P('pipe', 'expert')
- previous_grad: bfloat16 [4, 8192, 3584], P('pipe', 'expert')
The draws below stay inside these ranges and needn't reach their ends.
Inputs may be any that keep to these rules, and one draw needn't show every extreme that they name: `forward_route`: each token is routed to exactly one expert. Among the 128 tokens of one device no expert is named more than 12 times, and in some device's tokens one expert is named exactly 12 times. `backward_route`: as forward_route.
All inputs are finite; a program needn't handle non-finite values.
Results may differ from the reference program's by a relative error of at most 0.0066.
Values may be sent and summed in bfloat16 or wider, within the bound.
No kernel may reach another device: no remote copies, remote signals or barrier semaphores. Data moves between devices by JAX's collectives and lax.ppermute only.
A program may use at most 192 MiB of HBM per device.

```python
import math
import jax
import jax.numpy as jnp
import numpy as np
from jax import lax

D = 3584
HID = 1024
HD = 256
TOP = 1
TOK = 128
EXPERTS = 16
CAP = 12
TOKENS = 8192
N_PIPE = 4
N_EXPERT = 64


def levels(own_key, extent, cuts, least, high):
    loudness, own = 1.0, jax.random.fold_in(own_key, 6)
    for dim, blocks in cuts:
        draws = jnp.exp(jax.random.uniform(jax.random.fold_in(own, dim), (blocks,), jnp.float32, least / len(cuts), high / len(cuts)))
        loudness = loudness * jnp.repeat(draws, extent[dim] // blocks).reshape([-1 if axis == dim else 1 for axis in range(len(extent))])
    return loudness


def routed_block(stream_key, own, number, rows, amount, top, most, lean):
    order = jax.random.permutation(stream_key, amount)
    crowded, ordinary = load_shares(amount, rows * top, most, lean, True), load_shares(amount, rows * top, most, lean, False)
    places = jnp.arange(amount)

    def named(lengths, turn):
        used = int((lengths > 0).sum())
        fixed = max(1, used // 4)
        shifted = fixed + (places - fixed + turn * (used - fixed)) % max(1, amount - fixed)
        return jnp.zeros((amount,), jnp.int32).at[order[jnp.where(places < fixed, places, shifted)]].set(jnp.asarray(lengths, jnp.int32))

    lengths = jnp.where(number % 4 == 0, named(crowded, number // 4), named(ordinary, number - number // 4 - 1))
    mixed = jax.random.permutation(jax.random.fold_in(own, 3), amount)
    donor, receiver = mixed[0:amount // 2 * 2:2], mixed[1:amount // 2 * 2:2]
    room = jnp.minimum(lengths[donor] - 1, most - lengths[receiver]) // 2
    room = jnp.where((donor == order[0]) | (receiver == order[0]) | (lengths[receiver] == 0), 0, jnp.maximum(room, 0))
    shifted = jax.random.randint(jax.random.fold_in(own, 4), (amount // 2,), 0, 1 << 20) % (room + 1)
    lengths = lengths.at[donor].add(-shifted).at[receiver].add(shifted)
    items = jnp.searchsorted(jnp.cumsum(lengths), jnp.arange(rows * top), side="right").astype(jnp.int32)
    table = items.reshape(top, rows).T
    table = table[jax.random.permutation(jax.random.fold_in(own, 1), rows)]
    turn = jax.random.randint(jax.random.fold_in(own, 2), (rows, 1), 0, top)
    return jnp.take_along_axis(table, (jnp.arange(top)[None, :] + turn) % top, axis=1)


def load_shares(number_of, total, most, lean, full):
    weights = [(1 << 20) // math.isqrt(grade ** lean) + 1 for grade in range(1, number_of + 1)]
    largest = most if full else min(most, max(-(-total // number_of), total * weights[0] // sum(weights)))
    least = 1 if total - largest >= number_of - 1 else 0
    holding, rest = [largest] + [least] * (number_of - 1), total - largest - least * (number_of - 1)
    while rest > 0:
        free = [i for i in range(1, number_of) if holding[i] < largest] or [i for i in range(1, number_of) if holding[i] < most]
        mass, left = sum([weights[i] for i in free]), rest
        for i in free:
            extra = min(most - holding[i], max(1, left * weights[i] // mass), rest)
            holding[i] = holding[i] + extra
            rest = rest - extra
    return np.array(holding)


def noise(rng, extent, scale, reach, cuts=(), kind=jnp.bfloat16):
    entries = jax.random.normal(rng, extent, jnp.float32) * scale
    if len(cuts) > 0:
        entries = levels(rng, extent, cuts, -0.22, 0.18) * entries
    return jnp.clip(entries, min=-reach, max=reach).astype(kind)


def setup_inputs(seed: int = 0) -> dict:
    streams_of = jax.random.split(jax.random.key(seed), 12)
    forward_input = noise(streams_of[0], (N_PIPE, TOKENS, D), 1.0, 6.0, ((0, 4), (1, 64)))
    forward_route_keys = jax.random.split(jax.random.fold_in(streams_of[1], 1), N_PIPE * TOKENS // TOK)
    forward_route_turns = jax.random.permutation(jax.random.fold_in(streams_of[1], 3), N_PIPE * TOKENS // TOK)
    forward_route = jax.vmap(lambda own, number: routed_block(jax.random.fold_in(streams_of[1], 2), own, number, TOK, EXPERTS, TOP, CAP, 2))(forward_route_keys, forward_route_turns).reshape((N_PIPE, TOKENS, TOP))
    forward_weight = jnp.clip(jnp.exp(math.log(3.0) - 2.3025851 * jax.random.uniform(streams_of[2], (N_PIPE, TOKENS, TOP), jnp.float32) ** levels(streams_of[2], (N_PIPE, TOKENS, TOP), ((0, 4), (1, 64)), -0.2, 0.2)), 0.3, 3.0)
    backward_input = noise(streams_of[3], (N_PIPE, TOKENS, D), 1.0, 6.0, ((0, 4), (1, 64)))
    backward_route_keys = jax.random.split(jax.random.fold_in(streams_of[4], 1), N_PIPE * TOKENS // TOK)
    backward_route_turns = jax.random.permutation(jax.random.fold_in(streams_of[4], 3), N_PIPE * TOKENS // TOK)
    backward_route = jax.vmap(lambda own, number: routed_block(jax.random.fold_in(streams_of[4], 2), own, number, TOK, EXPERTS, TOP, CAP, 2))(backward_route_keys, backward_route_turns).reshape((N_PIPE, TOKENS, TOP))
    backward_weight = jnp.clip(jnp.exp(math.log(3.0) - 2.3025851 * jax.random.uniform(streams_of[5], (N_PIPE, TOKENS, TOP), jnp.float32) ** levels(streams_of[5], (N_PIPE, TOKENS, TOP), ((0, 4), (1, 64)), -0.2, 0.2)), 0.3, 3.0)
    output_grad = noise(streams_of[6], (N_PIPE, TOKENS, D), 1.0, 6.0, ((0, 4), (1, 64)))
    norm_gain = jnp.clip(1.0 + 0.18 * jax.random.normal(streams_of[7], (N_PIPE, D), jnp.float32), 0.1, 1.9)
    gate_weight = noise(streams_of[8], (N_PIPE, D, EXPERTS * HID), D ** -0.5, 0.09375, ((0, 4), (2, 64)))
    up_weight = noise(streams_of[9], (N_PIPE, D, EXPERTS * HID), D ** -0.5, 0.09375, ((0, 4), (2, 64)))
    down_weight = noise(streams_of[10], (N_PIPE, EXPERTS * HID, D), HID ** -0.5, 0.1875, ((0, 4), (1, 64)))
    return dict(forward_input=forward_input, forward_route=forward_route, forward_weight=forward_weight, backward_input=backward_input, backward_route=backward_route, backward_weight=backward_weight, output_grad=output_grad, norm_gain=norm_gain, gate_weight=gate_weight, up_weight=up_weight, down_weight=down_weight)


EPS = 1e-06

def normalize(values, gain):
    widened = values.astype(jnp.float32)
    scale = lax.rsqrt(lax.optimization_barrier(jnp.mean(widened * widened, axis=-1, keepdims=True)) + EPS)
    return (widened, scale, (widened * scale * gain).astype(jnp.bfloat16))

def rounded_sum(terms):
    return lax.optimization_barrier(jnp.sum(lax.optimization_barrier(terms.astype(jnp.bfloat16)).astype(jnp.float32), axis=1))

def one_section(inputs):
    forward_input, forward_route, forward_weight, backward_input, backward_route, backward_weight, output_grad, norm_gain, gate_weight, up_weight, down_weight = inputs
    blocks = HID // HD
    limit = N_EXPERT * CAP
    pairs = TOKENS * TOP
    ahead_wide, ahead_scale, ahead_normed = normalize(forward_input, norm_gain)
    behind_wide, behind_scale, behind_normed = normalize(backward_input, norm_gain)
    zero_row = jnp.zeros((1, D), jnp.bfloat16)
    ahead_table = jnp.concatenate([ahead_normed, zero_row], axis=0)
    behind_table = jnp.concatenate([behind_normed, zero_row], axis=0)
    cotangent = output_grad.astype(jnp.float32)
    routed_grad = (jnp.repeat(cotangent, TOP, axis=0) * backward_weight.reshape(-1)[:, None]).astype(jnp.bfloat16)
    grad_table = jnp.concatenate([routed_grad, zero_row], axis=0)
    ahead_routes = forward_route.reshape(-1)
    behind_routes = backward_route.reshape(-1)

    def per_expert(carry, expert):
        ahead_values, behind_values = carry
        ahead_index = jnp.nonzero(ahead_routes == expert, size=limit, fill_value=pairs)[0].astype(jnp.int32)
        behind_index = jnp.nonzero(behind_routes == expert, size=limit, fill_value=pairs)[0].astype(jnp.int32)
        start = (expert * HID).astype(jnp.int32)
        gate_cols = lax.dynamic_slice_in_dim(gate_weight, start, HID, 1)
        up_cols = lax.dynamic_slice_in_dim(up_weight, start, HID, 1)
        down_rows = lax.dynamic_slice_in_dim(down_weight, start, HID, 0)
        down_blocks = down_rows.astype(jnp.float32).reshape(blocks, HD, D)
        gate_blocks = gate_cols.astype(jnp.float32).reshape(D, blocks, HD)
        up_blocks = up_cols.astype(jnp.float32).reshape(D, blocks, HD)
        chosen = ahead_table[ahead_index // TOP]
        gate_pre = jnp.dot(chosen, gate_cols, preferred_element_type=jnp.float32)
        up_pre = jnp.dot(chosen, up_cols, preferred_element_type=jnp.float32)
        hidden = (jax.nn.silu(gate_pre) * up_pre).astype(jnp.bfloat16)
        parts = jnp.einsum('rgk,gkd->rgd', hidden.astype(jnp.float32).reshape(limit, blocks, HD), down_blocks)
        ahead_values = ahead_values.at[ahead_index].set(rounded_sum(parts), mode='drop')
        picked = behind_table[behind_index // TOP]
        grads = grad_table[behind_index]
        gate_back = jnp.dot(picked, gate_cols, preferred_element_type=jnp.float32)
        up_back = jnp.dot(picked, up_cols, preferred_element_type=jnp.float32)
        hidden_grad = jnp.dot(grads, down_rows.T, preferred_element_type=jnp.float32)
        sigmoid_gate = jax.nn.sigmoid(gate_back)
        gate_grad = (hidden_grad * up_back * sigmoid_gate * (1.0 + gate_back * (1.0 - sigmoid_gate))).astype(jnp.bfloat16)
        up_grad = (hidden_grad * gate_back * sigmoid_gate).astype(jnp.bfloat16)
        back = jnp.einsum('rgk,dgk->rgd', gate_grad.astype(jnp.float32).reshape(limit, blocks, HD), gate_blocks)
        back = back + jnp.einsum('rgk,dgk->rgd', up_grad.astype(jnp.float32).reshape(limit, blocks, HD), up_blocks)
        behind_values = behind_values.at[behind_index].set(rounded_sum(back), mode='drop')
        return ((ahead_values, behind_values), None)
    start_values = (jnp.zeros((pairs, D), jnp.float32), jnp.zeros((pairs, D), jnp.float32))
    (ahead_values, behind_values), _ = lax.scan(per_expert, start_values, jnp.arange(EXPERTS, dtype=jnp.int32))
    mixed = lax.optimization_barrier(jnp.sum(ahead_values.reshape(TOKENS, TOP, D) * forward_weight[:, :, None], axis=1))
    section_out = (ahead_wide + mixed).astype(jnp.bfloat16)
    normed_grad = lax.optimization_barrier(jnp.sum(behind_values.reshape(TOKENS, TOP, D), axis=1))
    unit = behind_wide * behind_scale
    unit_grad = norm_gain * normed_grad
    section_grad = cotangent + behind_scale * (unit_grad - unit * lax.optimization_barrier(jnp.mean(unit_grad * unit, axis=-1, keepdims=True)))
    return (section_out, section_grad.astype(jnp.bfloat16))

def reference(forward_input, forward_route, forward_weight, backward_input, backward_route, backward_weight, output_grad, norm_gain, gate_weight, up_weight, down_weight):
    section_out, section_grad = lax.map(one_section, (forward_input, forward_route, forward_weight, backward_input, backward_route, backward_weight, output_grad, norm_gain, gate_weight, up_weight, down_weight))
    return (jnp.roll(section_out, 1, axis=0), jnp.roll(section_grad, -1, axis=0))
```

```python
import jax
import jax.numpy as jnp
from jax import lax
from jax.sharding import PartitionSpec as P

EPS = 1e-06
XS, ZS, YS = 4, 8, 2
PAIRS = 4
EXPERTS = 16
BF = jnp.bfloat16
F32 = jnp.float32


def place(x, z, y):
    return (x % XS) * (ZS * YS) + (z % ZS) * YS + y


def hop(move):
    return [
        (place(x, z, y), place(*move(x, z, y)))
        for x in range(XS)
        for z in range(ZS)
        for y in range(YS)
    ]


def backwards(pairs):
    return [(b, a) for a, b in pairs]


Y_SWAP = hop(lambda x, z, y: (x, z, 1 - y))
Z_SWAP = hop(lambda x, z, y: (x, z ^ 1, y))
NEAR = hop(lambda x, z, y: (x, z - 1 if z % 2 == 0 else z + 1, y))
MIDDLE = hop(lambda x, z, y: (x, z + 2 if z % 2 == 0 else z - 2, y))
FAR = hop(lambda x, z, y: (x, z - 3 if z % 2 == 0 else z + 3, y))
OUTWARD = (NEAR, MIDDLE, FAR)
HOMEWARD = tuple(backwards(pairs) for pairs in OUTWARD)
X_GROUPS = [[place(x, z, y) for x in range(XS)] for z in range(ZS) for y in range(YS)]


def moved(array, pairs):
    return lax.ppermute(array, "expert", pairs)


def along_x(rows):
    count, width = rows.shape
    chunks = rows.reshape(XS, count // XS, width)
    chunks = lax.all_to_all(
        chunks, "expert", split_axis=0, concat_axis=0, tiled=True, axis_index_groups=X_GROUPS
    )
    return chunks.reshape(count, width)


def normalize(values, gain):
    widened = values.astype(F32)
    scale = lax.rsqrt(jnp.mean(widened * widened, axis=-1, keepdims=True) + EPS)
    return (widened, scale, (widened * scale * gain).astype(BF))


def slots_of(routes, capacity):
    flat = routes.reshape(-1)
    tokens = flat.shape[0]
    here = lax.axis_index("expert")
    z = (here // YS) % ZS
    pair, parity = z // 2, z % 2
    steps = (flat % PAIRS - pair) % PAIRS
    kind = jnp.where(
        steps == 0, 0, jnp.where(steps == 2, 3, jnp.where((steps == 1) == (parity == 1), 1, 2))
    )
    earlier = jnp.arange(tokens)[None, :] < jnp.arange(tokens)[:, None]
    rank = jnp.sum(((flat[:, None] == flat[None, :]) & earlier).astype(jnp.int32), axis=1)
    return ((flat // PAIRS) * PAIRS + kind) * capacity + rank


def swap_order(outer, inner, block):
    count = outer * inner * block
    row = jnp.arange(count)
    i, o, r = row // (outer * block), (row // block) % outer, row % block
    source = (o * inner + i) * block + r
    return (source[:, None] == jnp.arange(count)[None, :]).astype(BF)


def pick(onehot, rows):
    return jnp.dot(onehot, rows, preferred_element_type=F32).astype(BF)


def dispatch(slots, block):
    rows = along_x(slots)
    rows = pick(swap_order(XS, PAIRS, block), rows)
    size = XS * block
    kinds = [rows[i * size : (i + 1) * size] for i in range(PAIRS)]
    held = [kinds[0]] + [moved(kind, pairs) for kind, pairs in zip(kinds[1:], OUTWARD)]
    partner = [moved(kind, Z_SWAP) for kind in held]
    return jnp.concatenate(held + partner, axis=0)


def combine(parts, block):
    size = XS * block
    half = PAIRS * size
    back = []
    for i in range(PAIRS):
        mine = parts[i * size : (i + 1) * size]
        other = moved(parts[half + i * size : half + (i + 1) * size].astype(BF), Z_SWAP)
        total = (mine + other.astype(F32)).astype(BF)
        back.append(total if i == 0 else moved(total, HOMEWARD[i - 1]))
    rows = pick(swap_order(PAIRS, XS, block), jnp.concatenate(back, axis=0))
    return along_x(rows)


def expert_forward(rows, blocks):
    total = 0.0
    for gate_cols, up_cols, down_rows in blocks:
        gate_pre = jnp.dot(rows, gate_cols, preferred_element_type=F32)
        up_pre = jnp.dot(rows, up_cols, preferred_element_type=F32)
        hidden = (jax.nn.silu(gate_pre) * up_pre).astype(BF)
        total = total + jnp.dot(hidden, down_rows, preferred_element_type=F32)
    return total


def expert_backward(rows, grads, blocks):
    contract = (((1,), (1,)), ((), ()))
    total = 0.0
    for gate_cols, up_cols, down_rows in blocks:
        gate_back = jnp.dot(rows, gate_cols, preferred_element_type=F32)
        up_back = jnp.dot(rows, up_cols, preferred_element_type=F32)
        hidden_grad = lax.dot_general(grads, down_rows, contract, preferred_element_type=F32)
        sigmoid_gate = jax.nn.sigmoid(gate_back)
        gate_grad = (
            hidden_grad * up_back * sigmoid_gate * (1.0 + gate_back * (1.0 - sigmoid_gate))
        ).astype(BF)
        up_grad = (hidden_grad * gate_back * sigmoid_gate).astype(BF)
        total = total + lax.dot_general(gate_grad, gate_cols, contract, preferred_element_type=F32)
        total = total + lax.dot_general(up_grad, up_cols, contract, preferred_element_type=F32)
    return total


def per_device(
    forward_input,
    forward_route,
    forward_weight,
    backward_input,
    backward_route,
    backward_weight,
    output_grad,
    norm_gain,
    gate_weight,
    up_weight,
    down_weight,
):
    tokens = forward_input.shape[1]
    capacity = max(2, 3 * tokens // (2 * EXPERTS))
    count = EXPERTS * capacity
    gain = norm_gain[0]
    own = (gate_weight[0], up_weight[0], down_weight[0])
    blocks = (own, tuple(moved(weight, Y_SWAP) for weight in own))

    def onehot(routes):
        target = slots_of(routes, capacity)
        return (jnp.arange(count)[:, None] == target[None, :]).astype(BF)

    ahead_table, behind_table = onehot(forward_route[0]), onehot(backward_route[0])
    ahead_wide, ahead_scale, ahead_normed = normalize(forward_input[0], gain)
    behind_wide, behind_scale, behind_normed = normalize(backward_input[0], gain)
    cotangent = output_grad[0].astype(F32)
    routed_grad = (cotangent * backward_weight[0]).astype(BF)

    ahead_rows = dispatch(pick(ahead_table, ahead_normed), capacity)
    behind_rows = dispatch(pick(behind_table, behind_normed), capacity)
    grad_rows = dispatch(pick(behind_table, routed_grad), capacity)
    ahead_back = combine(expert_forward(ahead_rows, blocks), capacity)
    behind_back = combine(expert_backward(behind_rows, grad_rows, blocks), capacity)

    collect = (((0,), (0,)), ((), ()))
    mixed = lax.dot_general(ahead_table, ahead_back, collect, preferred_element_type=F32)
    section_out = (ahead_wide + mixed * forward_weight[0]).astype(BF)
    normed_grad = lax.dot_general(behind_table, behind_back, collect, preferred_element_type=F32)
    unit = behind_wide * behind_scale
    unit_grad = gain * normed_grad
    section_grad = cotangent + behind_scale * (
        unit_grad - unit * jnp.mean(unit_grad * unit, axis=-1, keepdims=True)
    )
    section_grad = section_grad.astype(BF)
    sections = lax.axis_size("pipe")
    ahead = [(i, (i + 1) % sections) for i in range(sections)]
    next_input = lax.ppermute(section_out, "pipe", ahead)
    previous_grad = lax.ppermute(section_grad, "pipe", backwards(ahead))
    return (next_input[None], previous_grad[None])


def solution(mesh):
    rows = P("pipe", "expert", None)
    columns = P("pipe", None, "expert")
    return jax.shard_map(
        per_device,
        mesh=mesh,
        in_specs=(rows,) * 7 + (P("pipe", None), columns, columns, rows),
        out_specs=(rows, rows),
        check_vma=False,
    )
```

```python
import jax
import jax.numpy as jnp
from jax import lax
from jax.experimental import pallas as pl
from jax.experimental.pallas import tpu as pltpu
from jax.sharding import PartitionSpec as P

EPS = 1e-06
XS, ZS, YS = 4, 8, 2
PAIRS = 4
EXPERTS = 16
BF = jnp.bfloat16
F32 = jnp.float32


def place(x, z, y):
    return (x % XS) * (ZS * YS) + (z % ZS) * YS + y


def hop(move):
    return [
        (place(x, z, y), place(*move(x, z, y)))
        for x in range(XS)
        for z in range(ZS)
        for y in range(YS)
    ]


def backwards(pairs):
    return [(b, a) for a, b in pairs]


Y_SWAP = hop(lambda x, z, y: (x, z, 1 - y))
Z_SWAP = hop(lambda x, z, y: (x, z ^ 1, y))
NEAR = hop(lambda x, z, y: (x, z - 1 if z % 2 == 0 else z + 1, y))
MIDDLE = hop(lambda x, z, y: (x, z + 2 if z % 2 == 0 else z - 2, y))
FAR = hop(lambda x, z, y: (x, z - 3 if z % 2 == 0 else z + 3, y))
OUTWARD = (NEAR, MIDDLE, FAR)
HOMEWARD = tuple(backwards(pairs) for pairs in OUTWARD)
X_GROUPS = [[place(x, z, y) for x in range(XS)] for z in range(ZS) for y in range(YS)]


def moved(array, pairs, name=None):
    if name is None:
        return lax.ppermute(array, "expert", pairs)
    with jax.named_scope(name):
        return lax.ppermute(array, "expert", pairs)


def along_x(rows):
    count, width = rows.shape
    chunks = rows.reshape(XS, count // XS, width)
    chunks = lax.all_to_all(
        chunks, "expert", split_axis=0, concat_axis=0, tiled=True, axis_index_groups=X_GROUPS
    )
    return chunks.reshape(count, width)


def normalize(values, gain):
    widened = values.astype(F32)
    scale = lax.rsqrt(jnp.mean(widened * widened, axis=-1, keepdims=True) + EPS)
    return (widened, scale, (widened * scale * gain).astype(BF))


def slots_of(routes, capacity):
    flat = routes.reshape(-1)
    tokens = flat.shape[0]
    here = lax.axis_index("expert")
    z = (here // YS) % ZS
    pair, parity = z // 2, z % 2
    steps = (flat % PAIRS - pair) % PAIRS
    kind = jnp.where(
        steps == 0, 0, jnp.where(steps == 2, 3, jnp.where((steps == 1) == (parity == 1), 1, 2))
    )
    earlier = jnp.arange(tokens)[None, :] < jnp.arange(tokens)[:, None]
    rank = jnp.sum(((flat[:, None] == flat[None, :]) & earlier).astype(jnp.int32), axis=1)
    x = flat // PAIRS
    steps = (here // (ZS * YS) - x) % XS
    return tuple(
        place * capacity + rank for place in (x * PAIRS + kind, kind * XS + x, steps * PAIRS + kind)
    )


def swap_order(outer, inner, block):
    count = outer * inner * block
    row = jnp.arange(count)
    i, o, r = row // (outer * block), (row // block) % outer, row % block
    source = (o * inner + i) * block + r
    return (source[:, None] == jnp.arange(count)[None, :]).astype(BF)


def pick(onehot, rows):
    return jnp.dot(onehot, rows, preferred_element_type=F32).astype(BF)


def after(done, later):
    return lax.optimization_barrier((done, later))[1]


def split(rows):
    size = rows.shape[0] // PAIRS
    return [rows[i * size : (i + 1) * size] for i in range(PAIRS)]


def outward(kinds, earlier, name):
    sent = [
        moved(kind if done is None else after(done, kind), pairs, name)
        for done, kind, pairs in zip(earlier, kinds[1:], OUTWARD)
    ]
    return [kinds[0]] + sent


def homeward(rows, name):
    kinds = split(rows)
    sent = [moved(kind, pairs, name) for kind, pairs in zip(kinds[1:], HOMEWARD)]
    return [kinds[0]] + sent


def added(mine, other):
    return (mine.astype(F32) + other.astype(F32)).astype(BF)


def mm(a, b):
    return jnp.dot(a, b, preferred_element_type=F32)


def mm_t(a, b):
    return lax.dot_general(a, b, (((1,), (1,)), ((), ())), preferred_element_type=F32)


def joined(refs):
    return jnp.concatenate([ref[...] for ref in refs], axis=0)


def stack_body(*refs):
    size = refs[0].shape[0]
    for i, ref in enumerate(refs[:-1]):
        refs[-1][i * size : (i + 1) * size, :] = ref[...]


def spread_body(mine, partner, order, out):
    size = out.shape[0] // (2 * XS)
    for half, rows in enumerate((mine, partner)):
        picked = mm(order[...], rows[...]).astype(BF)
        for x in range(XS):
            start = (2 * x + half) * size
            out[start : start + size, :] = picked[x * size : (x + 1) * size]


def sort_body(arrived, order, *outs):
    size = outs[0].shape[0]
    for half in range(2):
        chosen = [arrived[(2 * x + half) * size : (2 * x + half + 1) * size, :] for x in range(XS)]
        picked = mm(order[...], jnp.concatenate(chosen, axis=0)).astype(BF)
        for kind in range(PAIRS):
            outs[half * PAIRS + kind][...] = picked[kind * size : (kind + 1) * size]


def forward_body(rows, order, gate_a, up_a, down_a, gate_b, up_b, down_b, mine, partner):
    x = rows[...]
    total = None
    for gate_cols, up_cols, down_rows in ((gate_a, up_a, down_a), (gate_b, up_b, down_b)):
        gate_pre = mm(x, gate_cols[...])
        up_pre = mm(x, up_cols[...])
        hidden = (gate_pre / (1.0 + jnp.exp(-gate_pre)) * up_pre).astype(BF)
        part = mm(hidden, down_rows[...])
        total = part if total is None else total + part
    total = total.astype(BF)
    size = total.shape[0] // (2 * XS)
    for half, out in enumerate((mine, partner)):
        chosen = [total[(2 * x + half) * size : (2 * x + half + 1) * size] for x in range(XS)]
        out[...] = mm(order[...], jnp.concatenate(chosen, axis=0)).astype(BF)


def backward_body(
    rows, rows_p, grads, grads_p, gate_a, up_a, down_a, gate_b, up_b, down_b, mine, partner
):
    x = joined((rows, rows_p))
    g = joined((grads, grads_p))
    total = None
    for gate_cols, up_cols, down_rows in ((gate_a, up_a, down_a), (gate_b, up_b, down_b)):
        gate_back = mm(x, gate_cols[...])
        up_back = mm(x, up_cols[...])
        hidden_grad = mm_t(g, down_rows[...])
        sigmoid_gate = 1.0 / (1.0 + jnp.exp(-gate_back))
        gate_grad = (
            hidden_grad * up_back * sigmoid_gate * (1.0 + gate_back * (1.0 - sigmoid_gate))
        ).astype(BF)
        up_grad = (hidden_grad * gate_back * sigmoid_gate).astype(BF)
        part = mm_t(gate_grad, gate_cols[...]) + mm_t(up_grad, up_cols[...])
        total = part if total is None else total + part
    half = mine.shape[0]
    mine[...] = total[:half].astype(BF)
    partner[...] = total[half:].astype(BF)


def on_core(body, rows, outs, *operands):
    shape = jax.ShapeDtypeStruct((rows, operands[0].shape[1]), BF)
    whole = pl.BlockSpec(memory_space=pltpu.VMEM)
    return pl.pallas_call(
        body,
        out_shape=(shape,) * outs,
        in_specs=[whole] * len(operands),
        out_specs=(whole,) * outs,
        compiler_params=pltpu.CompilerParams(vmem_limit_bytes=56 * 1024 * 1024),
        cost_estimate=pl.CostEstimate(flops=1000, bytes_accessed=1000, transcendentals=0),
    )(*operands)


def stacked(kinds):
    return on_core(stack_body, PAIRS * kinds[0].shape[0], 1, *kinds)[0]


def to_section(rows, block):
    count = rows.shape[0]
    here = lax.axis_index("expert") // (ZS * YS)
    row = jnp.arange(count)
    step, kind, rank = row // (PAIRS * block), (row // block) % PAIRS, row % block
    source = (kind * XS + (here + step) % XS) * block + rank
    chunks = split(pick((source[:, None] == row[None, :]).astype(BF), rows))
    sections, devices = lax.axis_size("pipe"), XS * ZS * YS
    arrived = []
    for step in (2, 1, 3, 0):
        pairs = [
            (s * devices + a, (s - 1) % sections * devices + b)
            for s in range(sections)
            for a, b in hop(lambda x, z, y: (x + step, z, y))
        ]
        with jax.named_scope("behind_section"):
            arrived.append(lax.ppermute(chunks[step], ("pipe", "expert"), pairs))
    arrived = [arrived[i] for i in (3, 1, 0, 2)]
    return jnp.concatenate(arrived, axis=0)


def per_device(
    forward_input,
    forward_route,
    forward_weight,
    backward_input,
    backward_route,
    backward_weight,
    output_grad,
    norm_gain,
    gate_weight,
    up_weight,
    down_weight,
):
    tokens = forward_input.shape[1]
    capacity = max(2, 3 * tokens // (2 * EXPERTS))
    count = EXPERTS * capacity
    gain = norm_gain[0]
    own = (gate_weight[0], up_weight[0], down_weight[0])

    def onehot(target):
        return (jnp.arange(count)[:, None] == target[None, :]).astype(BF)

    ahead_table, ahead_first, _ = (onehot(target) for target in slots_of(forward_route[0], capacity))
    behind_table, _, _ = (onehot(target) for target in slots_of(backward_route[0], capacity))
    sections = lax.axis_size("pipe")
    ahead = [(i, (i + 1) % sections) for i in range(sections)]
    ahead_wide, ahead_scale, ahead_normed = normalize(forward_input[0], gain)
    behind_wide, behind_scale, behind_normed = normalize(backward_input[0], gain)
    routed_grad = (output_grad[0].astype(F32) * backward_weight[0]).astype(BF)

    to_x, to_class = swap_order(PAIRS, XS, capacity), swap_order(XS, PAIRS, capacity)
    gate_other = moved(own[0], Y_SWAP, "gate_swap")
    up_other = moved(after(gate_other, own[1]), Y_SWAP, "up_swap")
    down_other = moved(after(up_other, own[2]), Y_SWAP, "down_swap")
    weights = own + (gate_other, up_other, down_other)

    ahead_held = outward(split(pick(ahead_first, ahead_normed)), (None,) * 3, "ahead_outward")
    behind_both = on_core(
        spread_body, 2 * count, 1, behind_normed, routed_grad, behind_table
    )[0]
    kinds = on_core(sort_body, count // PAIRS, 2 * PAIRS, along_x(behind_both), to_class)
    behind_held = outward(kinds[:PAIRS], ahead_held[1:], "behind_outward")
    grad_held = outward(kinds[PAIRS:], behind_held[1:], "grad_outward")

    ahead_mine = jnp.concatenate(ahead_held, axis=0)
    ahead_partner = moved(ahead_mine, Z_SWAP, "ahead_pair")
    behind_mine = jnp.concatenate(behind_held, axis=0)
    behind_partner = moved(after(ahead_partner, behind_mine), Z_SWAP, "behind_pair")
    grad_mine = jnp.concatenate(grad_held, axis=0)
    grad_partner = moved(after(behind_partner, grad_mine), Z_SWAP, "grad_pair")

    ahead_partner = after(kinds, ahead_partner)
    ahead_both = along_x(on_core(spread_body, 2 * count, 1, ahead_mine, ahead_partner, to_x)[0])
    ahead_mine, ahead_partner = on_core(forward_body, count, 2, ahead_both, to_class, *weights)
    ahead_other = moved(ahead_partner, Z_SWAP, "ahead_pair_sum")
    behind_mine, behind_partner = on_core(
        backward_body, count, 2, after(ahead_mine, behind_mine), behind_partner, grad_mine,
        grad_partner, *weights
    )
    ahead_home = homeward(added(ahead_mine, ahead_other), "ahead_homeward")
    behind_partner = after(ahead_other, behind_partner)
    behind_other = moved(behind_partner, Z_SWAP, "behind_pair_sum")
    behind_home = homeward(added(behind_mine, behind_other), "behind_homeward")
    ahead_back = along_x(pick(to_x, jnp.concatenate(ahead_home, axis=0)))
    behind_back = to_section(jnp.concatenate(behind_home, axis=0), capacity)

    with jax.named_scope("behind_late"):
        late_rows = jnp.concatenate([backward_input[0], output_grad[0]], axis=0)
        late_rows = lax.ppermute(after(down_other, late_rows), "pipe", backwards(ahead))
        late_small = jnp.zeros((2, gain.shape[0]), F32).at[0].set(gain)
        late_small = late_small.at[1, :tokens].set(backward_route[0, :, 0].astype(F32))
        late_small = lax.ppermute(after(down_other, late_small), "pipe", backwards(ahead))
    collect = (((0,), (0,)), ((), ()))
    mixed = lax.dot_general(ahead_table, ahead_back, collect, preferred_element_type=F32)
    section_out = (ahead_wide + mixed * forward_weight[0]).astype(BF)
    next_input = lax.ppermute(section_out, "pipe", ahead)
    late_gain, late_route = late_small[0], late_small[1, :tokens].astype(jnp.int32)
    late_table = onehot(slots_of(late_route, capacity)[2])
    normed_grad = lax.dot_general(late_table, behind_back, collect, preferred_element_type=F32)
    late_wide, late_scale, _ = normalize(late_rows[:tokens], late_gain)
    unit = late_wide * late_scale
    unit_grad = late_gain * normed_grad
    previous_grad = late_rows[tokens:].astype(F32) + late_scale * (
        unit_grad - unit * jnp.mean(unit_grad * unit, axis=-1, keepdims=True)
    )
    return (next_input[None], previous_grad.astype(BF)[None])


def solution(mesh):
    rows = P("pipe", "expert", None)
    columns = P("pipe", None, "expert")
    return jax.shard_map(
        per_device,
        mesh=mesh,
        in_specs=(rows,) * 7 + (P("pipe", None), columns, columns, rows),
        out_specs=(rows, rows),
        check_vma=False,
    )
```

```python
import jax
import jax.numpy as jnp
from jax import lax
from jax.experimental import pallas as pl
from jax.experimental.pallas import tpu as pltpu
from jax.sharding import PartitionSpec as P

EPS = 1e-06
XS, ZS, YS = 4, 8, 2
PAIRS = 4
EXPERTS = 16
BF = jnp.bfloat16
F32 = jnp.float32
COSTS = (5_000_000_000, 15_000_000_000, 5_000_000_000, 40_000_000_000, 5_000_000_000, 40_000_000_000)


def place(x, z, y):
    return (x % XS) * (ZS * YS) + (z % ZS) * YS + y


def hop(move):
    return [
        (place(x, z, y), place(*move(x, z, y)))
        for x in range(XS)
        for z in range(ZS)
        for y in range(YS)
    ]


def backwards(pairs):
    return [(b, a) for a, b in pairs]


Y_SWAP = hop(lambda x, z, y: (x, z, 1 - y))
Z_SWAP = hop(lambda x, z, y: (x, z ^ 1, y))
NEAR = hop(lambda x, z, y: (x, z - 1 if z % 2 == 0 else z + 1, y))
MIDDLE = hop(lambda x, z, y: (x, z + 2 if z % 2 == 0 else z - 2, y))
FAR = hop(lambda x, z, y: (x, z - 3 if z % 2 == 0 else z + 3, y))
OUTWARD = (NEAR, MIDDLE, FAR)
HOMEWARD = tuple(backwards(pairs) for pairs in OUTWARD)
X_GROUPS = [[place(x, z, y) for x in range(XS)] for z in range(ZS) for y in range(YS)]


def moved(array, pairs, name=None):
    if name is None:
        return lax.ppermute(array, "expert", pairs)
    with jax.named_scope(name):
        return lax.ppermute(array, "expert", pairs)


def along_x(rows):
    count, width = rows.shape
    chunks = rows.reshape(XS, count // XS, width)
    chunks = lax.all_to_all(
        chunks, "expert", split_axis=0, concat_axis=0, tiled=True, axis_index_groups=X_GROUPS
    )
    return chunks.reshape(count, width)


def normalize(values):
    widened = values.astype(F32)
    scale = lax.rsqrt(jnp.mean(widened * widened, axis=-1, keepdims=True) + EPS)
    return (widened, scale)


def slots_of(routes, capacity):
    flat = routes.reshape(-1)
    tokens = flat.shape[0]
    here = lax.axis_index("expert")
    z = (here // YS) % ZS
    pair, parity = z // 2, z % 2
    steps = (flat % PAIRS - pair) % PAIRS
    kind = jnp.where(
        steps == 0, 0, jnp.where(steps == 2, 3, jnp.where((steps == 1) == (parity == 1), 1, 2))
    )
    earlier = jnp.arange(tokens)[None, :] < jnp.arange(tokens)[:, None]
    rank = jnp.sum(((flat[:, None] == flat[None, :]) & earlier).astype(jnp.int32), axis=1)
    x = flat // PAIRS
    steps = (here // (ZS * YS) - x) % XS
    return tuple(
        place * capacity + rank for place in (x * PAIRS + kind, kind * XS + x, steps * PAIRS + kind)
    )


def swap_order(outer, inner, block):
    count = outer * inner * block
    row = jnp.arange(count)
    i, o, r = row // (outer * block), (row // block) % outer, row % block
    source = (o * inner + i) * block + r
    return (source[:, None] == jnp.arange(count)[None, :]).astype(BF)


def pick(onehot, rows):
    return jnp.dot(onehot, rows, preferred_element_type=F32).astype(BF)


def after(done, later):
    return lax.optimization_barrier((done, later))[1]


def split(rows):
    size = rows.shape[0] // PAIRS
    return [rows[i * size : (i + 1) * size] for i in range(PAIRS)]


def outward(kinds, earlier, name):
    sent = [
        moved(after(done, kind), pairs, name)
        for done, kind, pairs in zip(earlier, kinds[1:], OUTWARD)
    ]
    return [kinds[0]] + sent


def paired(kinds, costs, before, name):
    size = kinds[0].shape[0]
    groups = [
        on_core(stack_body, 2 * size, 1, *kinds[2 * i : 2 * i + 2], cost=costs[i])[0]
        for i in range(2)
    ]
    near = moved(after(before, groups[0]), Z_SWAP, name)
    return groups, (near, moved(after(near, groups[1]), Z_SWAP, name))


def returned(mine, partner, before, name):
    size = mine[0].shape[0] // 2
    far_other = moved(after(before, partner[1]), Z_SWAP, name)
    near_other = moved(after(before, partner[0]), Z_SWAP, name)
    far = added(mine[1], far_other)
    near = added(mine[0], near_other)
    back = [
        near[:size],
        moved(near[size:], HOMEWARD[0], name),
        moved(far[:size], HOMEWARD[1], name),
        moved(far[size:], HOMEWARD[2], name),
    ]
    return jnp.concatenate(back, axis=0), (far_other, near_other)


def added(mine, other):
    return (mine.astype(F32) + other.astype(F32)).astype(BF)


def mm(a, b):
    return jnp.dot(a, b, preferred_element_type=F32)


def mm_t(a, b):
    return lax.dot_general(a, b, (((1,), (1,)), ((), ())), preferred_element_type=F32)


def joined(refs):
    return jnp.concatenate([ref[...] for ref in refs], axis=0)


def pick_body(values, gain, table, *outs):
    widened = values[...].astype(F32)
    scale = lax.rsqrt(jnp.mean(widened * widened, axis=-1, keepdims=True) + EPS)
    picked = mm(table[...], (widened * scale * gain[...]).astype(BF)).astype(BF)
    cut(picked, outs)


def cut(rows, outs):
    size = outs[0].shape[0]
    for i, out in enumerate(outs):
        out[...] = rows[i * size : (i + 1) * size]


def sort_body(arrived, order, *outs):
    cut(mm(order[...], arrived[...]).astype(BF), outs)


def stack_body(*refs):
    size = refs[0].shape[0]
    for i, ref in enumerate(refs[:-1]):
        refs[-1][i * size : (i + 1) * size, :] = ref[...]


def spread_body(own, near, middle, far, partner_a, partner_b, order, out):
    size = out.shape[0] // (2 * XS)
    for half, refs in enumerate(((own, near, middle, far), (partner_a, partner_b))):
        picked = mm(order[...], joined(refs)).astype(BF)
        for x in range(XS):
            start = (2 * x + half) * size
            out[start : start + size, :] = picked[x * size : (x + 1) * size]


def halves(rows, order):
    size = rows.shape[0] // (2 * XS)
    picked = []
    for half in range(2):
        chosen = [rows[(2 * x + half) * size : (2 * x + half + 1) * size] for x in range(XS)]
        picked.append(mm(order[...], jnp.concatenate(chosen, axis=0)).astype(BF))
    return picked


def forward_body(rows, order, gate_a, up_a, down_a, gate_b, up_b, down_b, *outs):
    x = rows[...]
    total = None
    for gate_cols, up_cols, down_rows in ((gate_a, up_a, down_a), (gate_b, up_b, down_b)):
        gate_pre = mm(x, gate_cols[...])
        up_pre = mm(x, up_cols[...])
        hidden = (gate_pre / (1.0 + jnp.exp(-gate_pre)) * up_pre).astype(BF)
        part = mm(hidden, down_rows[...])
        total = part if total is None else total + part
    for half, picked in enumerate(halves(total.astype(BF), order)):
        cut(picked, outs[2 * half : 2 * half + 2])


def backward_body(*refs):
    gate_a, up_a, down_a, gate_b, up_b, down_b = refs[12:18]
    x, g = joined(refs[:6]), joined(refs[6:12])
    total = None
    for gate_cols, up_cols, down_rows in ((gate_a, up_a, down_a), (gate_b, up_b, down_b)):
        gate_back = mm(x, gate_cols[...])
        up_back = mm(x, up_cols[...])
        hidden_grad = mm_t(g, down_rows[...])
        sigmoid_gate = 1.0 / (1.0 + jnp.exp(-gate_back))
        gate_grad = (
            hidden_grad * up_back * sigmoid_gate * (1.0 + gate_back * (1.0 - sigmoid_gate))
        ).astype(BF)
        up_grad = (hidden_grad * gate_back * sigmoid_gate).astype(BF)
        part = mm_t(gate_grad, gate_cols[...]) + mm_t(up_grad, up_cols[...])
        total = part if total is None else total + part
    cut(total.astype(BF), refs[18:])


def on_core(body, rows, outs, *operands, cost=0):
    shape = jax.ShapeDtypeStruct((rows, operands[0].shape[1]), BF)
    whole = pl.BlockSpec(memory_space=pltpu.VMEM)
    return pl.pallas_call(
        body,
        out_shape=(shape,) * outs,
        in_specs=[whole] * len(operands),
        out_specs=(whole,) * outs,
        compiler_params=pltpu.CompilerParams(vmem_limit_bytes=56 * 1024 * 1024),
        cost_estimate=pl.CostEstimate(flops=cost, bytes_accessed=0, transcendentals=0),
    )(*operands)


def to_section(rows, block, shift):
    count = rows.shape[0]
    here = lax.axis_index("expert") // (ZS * YS)
    row = jnp.arange(count)
    step, kind, rank = row // (PAIRS * block), (row // block) % PAIRS, row % block
    source = (kind * XS + (here + step) % XS) * block + rank
    chunks = split(pick((source[:, None] == row[None, :]).astype(BF), rows))
    sections, devices = lax.axis_size("pipe"), XS * ZS * YS
    arrived = []
    for step in (2, 1, 3, 0):
        pairs = [
            (s * devices + a, (s + shift) % sections * devices + b)
            for s in range(sections)
            for a, b in hop(lambda x, z, y: (x + step, z, y))
        ]
        with jax.named_scope("to_section"):
            arrived.append(lax.ppermute(chunks[step], ("pipe", "expert"), pairs))
    arrived = [arrived[i] for i in (3, 1, 0, 2)]
    return jnp.concatenate(arrived, axis=0)


def per_device(
    forward_input,
    forward_route,
    forward_weight,
    backward_input,
    backward_route,
    backward_weight,
    output_grad,
    norm_gain,
    gate_weight,
    up_weight,
    down_weight,
):
    tokens = forward_input.shape[1]
    capacity = max(2, 3 * tokens // (2 * EXPERTS))
    count = EXPERTS * capacity
    gain = norm_gain[0]
    own = (gate_weight[0], up_weight[0], down_weight[0])

    def onehot(target):
        return (jnp.arange(count)[:, None] == target[None, :]).astype(BF)

    ahead_table, ahead_first, _ = (onehot(target) for target in slots_of(forward_route[0], capacity))
    behind_table, _, _ = (onehot(target) for target in slots_of(backward_route[0], capacity))
    sections = lax.axis_size("pipe")
    ahead = [(i, (i + 1) % sections) for i in range(sections)]
    size = count // PAIRS
    ahead_kinds = on_core(pick_body, size, PAIRS, forward_input[0], norm_gain, ahead_first)
    behind_wide, behind_scale = normalize(backward_input[0])
    behind_normed = (behind_wide * behind_scale * gain).astype(BF)
    routed_grad = (output_grad[0].astype(F32) * backward_weight[0]).astype(BF)
    to_x, to_class = swap_order(PAIRS, XS, capacity), swap_order(XS, PAIRS, capacity)
    gate_other = moved(own[0], Y_SWAP, "gate_swap")
    up_other = moved(after(gate_other, own[1]), Y_SWAP, "up_swap")
    down_other = moved(after(up_other, own[2]), Y_SWAP, "down_swap")
    weights = own + (gate_other, up_other, down_other)

    behind_slots, grad_slots = pick(behind_table, behind_normed), pick(behind_table, routed_grad)
    behind_kinds = on_core(sort_body, size, PAIRS, along_x(behind_slots), to_class)
    grad_kinds = on_core(sort_body, size, PAIRS, along_x(grad_slots), to_class)
    ahead_held = outward(ahead_kinds, (gain,) * 3, "ahead_outward")
    (near, far), ahead_rows = paired(ahead_held, COSTS[:2], gain, "ahead_pair")
    behind_held = outward(behind_kinds, (near, far, far), "behind_outward")
    behind_held[1] = after(gate_other, behind_held[1])
    behind_held[3] = after(up_other, behind_held[3])
    (near, far), behind_rows = paired(behind_held, COSTS[2:4], ahead_rows[1], "behind_pair")
    grad_held = outward(grad_kinds, (near, far, far), "grad_outward")
    grad_held[3] = after(down_other, grad_held[3])
    _, grad_rows = paired(grad_held, COSTS[4:], behind_rows[1], "grad_pair")

    ahead_both = along_x(on_core(spread_body, 2 * count, 1, *ahead_held, *ahead_rows, to_x)[0])
    ahead_parts = on_core(forward_body, count // 2, 4, ahead_both, to_class, *weights)
    behind_parts = on_core(
        backward_body, count // 2, 4, *behind_held, *behind_rows, *grad_held, *grad_rows[:1],
        after(ahead_parts, grad_rows[1]), *weights
    )
    ahead_home, others = returned(ahead_parts[:2], ahead_parts[2:], gain, "ahead_return")
    behind_home, _ = returned(behind_parts[:2], behind_parts[2:], others, "behind_return")
    ahead_back = along_x(pick(to_x, ahead_home))

    with jax.named_scope("behind_late"):
        late_rows = jnp.concatenate([backward_input[0], output_grad[0]], axis=0)
        late_rows = lax.ppermute(after(down_other, late_rows), "pipe", backwards(ahead))
        late_small = jnp.zeros((2, gain.shape[0]), F32).at[0].set(gain)
        late_small = late_small.at[1, :tokens].set(backward_route[0, :, 0].astype(F32))
        late_small = lax.ppermute(after(down_other, late_small), "pipe", backwards(ahead))
    collect = (((0,), (0,)), ((), ()))
    mixed = lax.dot_general(ahead_table, ahead_back, collect, preferred_element_type=F32)
    section_out = (forward_input[0].astype(F32) + mixed * forward_weight[0]).astype(BF)
    next_input = lax.ppermute(section_out, "pipe", ahead)
    behind_back = to_section(after(section_out, behind_home), capacity, -1)
    late_gain, late_route = late_small[0], late_small[1, :tokens].astype(jnp.int32)
    late_table = onehot(slots_of(late_route, capacity)[2])
    normed_grad = lax.dot_general(late_table, behind_back, collect, preferred_element_type=F32)
    late_wide, late_scale = normalize(late_rows[:tokens])
    unit = late_wide * late_scale
    unit_grad = late_gain * normed_grad
    previous_grad = late_rows[tokens:].astype(F32) + late_scale * (
        unit_grad - unit * jnp.mean(unit_grad * unit, axis=-1, keepdims=True)
    )
    return (next_input[None], previous_grad.astype(BF)[None])


def solution(mesh):
    rows = P("pipe", "expert", None)
    columns = P("pipe", None, "expert")
    return jax.shard_map(
        per_device,
        mesh=mesh,
        in_specs=(rows,) * 7 + (P("pipe", None), columns, columns, rows),
        out_specs=(rows, rows),
        check_vma=False,
    )
```

```python
import jax
import jax.numpy as jnp
from jax import lax
from jax.experimental import pallas as pl
from jax.experimental.pallas import tpu as pltpu
from jax.sharding import PartitionSpec as P

EPS = 1e-06
XS, ZS, YS = 4, 8, 2
PAIRS = 4
EXPERTS = 16
BF = jnp.bfloat16
F32 = jnp.float32
COSTS = (20_000_000_000, 15_000_000_000, 5_000_000_000, 40_000_000_000, 5_000_000_000, 40_000_000_000)


def place(x, z, y):
    return (x % XS) * (ZS * YS) + (z % ZS) * YS + y


def hop(move):
    return [
        (place(x, z, y), place(*move(x, z, y)))
        for x in range(XS)
        for z in range(ZS)
        for y in range(YS)
    ]


def backwards(pairs):
    return [(b, a) for a, b in pairs]


Y_SWAP = hop(lambda x, z, y: (x, z, 1 - y))
Z_SWAP = hop(lambda x, z, y: (x, z ^ 1, y))
NEAR = hop(lambda x, z, y: (x, z - 1 if z % 2 == 0 else z + 1, y))
MIDDLE = hop(lambda x, z, y: (x, z + 2 if z % 2 == 0 else z - 2, y))
FAR = hop(lambda x, z, y: (x, z - 3 if z % 2 == 0 else z + 3, y))
OUTWARD = (NEAR, MIDDLE, FAR)
HOMEWARD = tuple(backwards(pairs) for pairs in OUTWARD)
X_GROUPS = [[place(x, z, y) for x in range(XS)] for z in range(ZS) for y in range(YS)]


def moved(array, pairs, name=None):
    if name is None:
        return lax.ppermute(array, "expert", pairs)
    with jax.named_scope(name):
        return lax.ppermute(array, "expert", pairs)


def along_x(rows):
    count, width = rows.shape
    chunks = rows.reshape(XS, count // XS, width)
    chunks = lax.all_to_all(
        chunks, "expert", split_axis=0, concat_axis=0, tiled=True, axis_index_groups=X_GROUPS
    )
    return chunks.reshape(count, width)


def normalize(values):
    widened = values.astype(F32)
    scale = lax.rsqrt(jnp.mean(widened * widened, axis=-1, keepdims=True) + EPS)
    return (widened, scale)


def slots_of(routes, capacity):
    flat = routes.reshape(-1)
    tokens = flat.shape[0]
    here = lax.axis_index("expert")
    z = (here // YS) % ZS
    pair, parity = z // 2, z % 2
    steps = (flat % PAIRS - pair) % PAIRS
    kind = jnp.where(
        steps == 0, 0, jnp.where(steps == 2, 3, jnp.where((steps == 1) == (parity == 1), 1, 2))
    )
    earlier = jnp.arange(tokens)[None, :] < jnp.arange(tokens)[:, None]
    rank = jnp.sum(((flat[:, None] == flat[None, :]) & earlier).astype(jnp.int32), axis=1)
    x = flat // PAIRS
    steps = (here // (ZS * YS) - x) % XS
    return tuple(
        place * capacity + rank for place in (x * PAIRS + kind, kind * XS + x, steps * PAIRS + kind)
    )


def swap_order(outer, inner, block):
    count = outer * inner * block
    row = jnp.arange(count)
    i, o, r = row // (outer * block), (row // block) % outer, row % block
    source = (o * inner + i) * block + r
    return (source[:, None] == jnp.arange(count)[None, :]).astype(BF)


def pick(onehot, rows):
    return jnp.dot(onehot, rows, preferred_element_type=F32).astype(BF)


def after(done, later):
    return lax.optimization_barrier((done, later))[1]


def split(rows):
    size = rows.shape[0] // PAIRS
    return [rows[i * size : (i + 1) * size] for i in range(PAIRS)]


def outward(kinds, earlier, name):
    sent = [
        moved(after(done, kind), pairs, name)
        for done, kind, pairs in zip(earlier, kinds[1:], OUTWARD)
    ]
    return [kinds[0]] + sent


def paired(kinds, costs, before, name):
    size = kinds[0].shape[0]
    groups = [
        on_core(stack_body, 2 * size, 1, *kinds[2 * i : 2 * i + 2], cost=costs[i])[0]
        for i in range(2)
    ]
    near = moved(after(before, groups[0]), Z_SWAP, name)
    return groups, (near, moved(after(near, groups[1]), Z_SWAP, name))


def returned(mine, partner, before, name):
    size = mine[0].shape[0] // 2
    far_other = moved(after(before, partner[1]), Z_SWAP, name)
    near_other = moved(after(before, partner[0]), Z_SWAP, name)
    far = added(mine[1], far_other)
    near = added(mine[0], near_other)
    back = [
        near[:size],
        moved(near[size:], HOMEWARD[0], name),
        moved(far[:size], HOMEWARD[1], name),
        moved(far[size:], HOMEWARD[2], name),
    ]
    return jnp.concatenate(back, axis=0), (far_other, near_other)


def added(mine, other):
    return (mine.astype(F32) + other.astype(F32)).astype(BF)


def mm(a, b):
    return jnp.dot(a, b, preferred_element_type=F32)


def mm_t(a, b):
    return lax.dot_general(a, b, (((1,), (1,)), ((), ())), preferred_element_type=F32)


def joined(refs):
    return jnp.concatenate([ref[...] for ref in refs], axis=0)


def pick_body(values, gain, table, *outs):
    widened = values[...].astype(F32)
    scale = lax.rsqrt(jnp.mean(widened * widened, axis=-1, keepdims=True) + EPS)
    picked = mm(table[...], (widened * scale * gain[...]).astype(BF)).astype(BF)
    cut(picked, outs)


def cut(rows, outs):
    size = outs[0].shape[0]
    for i, out in enumerate(outs):
        out[...] = rows[i * size : (i + 1) * size]


def sort_body(arrived, order, *outs):
    cut(mm(order[...], arrived[...]).astype(BF), outs)


def stack_body(*refs):
    size = refs[0].shape[0]
    for i, ref in enumerate(refs[:-1]):
        refs[-1][i * size : (i + 1) * size, :] = ref[...]


def spread_body(own, near, middle, far, partner_a, partner_b, order, out):
    size = out.shape[0] // (2 * XS)
    for half, refs in enumerate(((own, near, middle, far), (partner_a, partner_b))):
        picked = mm(order[...], joined(refs)).astype(BF)
        for x in range(XS):
            start = (2 * x + half) * size
            out[start : start + size, :] = picked[x * size : (x + 1) * size]


def halves(rows, order):
    size = rows.shape[0] // (2 * XS)
    picked = []
    for half in range(2):
        chosen = [rows[(2 * x + half) * size : (2 * x + half + 1) * size] for x in range(XS)]
        picked.append(mm(order[...], jnp.concatenate(chosen, axis=0)).astype(BF))
    return picked


def forward_body(rows, order, gate_a, up_a, down_a, gate_b, up_b, down_b, *outs):
    x = rows[...]
    total = None
    for gate_cols, up_cols, down_rows in ((gate_a, up_a, down_a), (gate_b, up_b, down_b)):
        gate_pre = mm(x, gate_cols[...])
        up_pre = mm(x, up_cols[...])
        hidden = (gate_pre / (1.0 + jnp.exp(-gate_pre)) * up_pre).astype(BF)
        part = mm(hidden, down_rows[...])
        total = part if total is None else total + part
    for half, picked in enumerate(halves(total.astype(BF), order)):
        cut(picked, outs[2 * half : 2 * half + 2])


def backward_body(*refs):
    gate_a, up_a, down_a, gate_b, up_b, down_b = refs[12:18]
    x, g = joined(refs[:6]), joined(refs[6:12])
    total = None
    for gate_cols, up_cols, down_rows in ((gate_a, up_a, down_a), (gate_b, up_b, down_b)):
        gate_back = mm(x, gate_cols[...])
        up_back = mm(x, up_cols[...])
        hidden_grad = mm_t(g, down_rows[...])
        sigmoid_gate = 1.0 / (1.0 + jnp.exp(-gate_back))
        gate_grad = (
            hidden_grad * up_back * sigmoid_gate * (1.0 + gate_back * (1.0 - sigmoid_gate))
        ).astype(BF)
        up_grad = (hidden_grad * gate_back * sigmoid_gate).astype(BF)
        part = mm_t(gate_grad, gate_cols[...]) + mm_t(up_grad, up_cols[...])
        total = part if total is None else total + part
    cut(total.astype(BF), refs[18:])


def on_core(body, rows, outs, *operands, cost=0):
    shape = jax.ShapeDtypeStruct((rows, operands[0].shape[1]), BF)
    whole = pl.BlockSpec(memory_space=pltpu.VMEM)
    return pl.pallas_call(
        body,
        out_shape=(shape,) * outs,
        in_specs=[whole] * len(operands),
        out_specs=(whole,) * outs,
        compiler_params=pltpu.CompilerParams(vmem_limit_bytes=56 * 1024 * 1024),
        cost_estimate=pl.CostEstimate(flops=cost, bytes_accessed=0, transcendentals=0),
    )(*operands)


def to_section(rows, block, shift):
    count = rows.shape[0]
    here = lax.axis_index("expert") // (ZS * YS)
    row = jnp.arange(count)
    step, kind, rank = row // (PAIRS * block), (row // block) % PAIRS, row % block
    source = (kind * XS + (here + step) % XS) * block + rank
    chunks = split(pick((source[:, None] == row[None, :]).astype(BF), rows))
    sections, devices = lax.axis_size("pipe"), XS * ZS * YS
    arrived = []
    for step in (2, 1, 3, 0):
        pairs = [
            (s * devices + a, (s + shift) % sections * devices + b)
            for s in range(sections)
            for a, b in hop(lambda x, z, y: (x + step, z, y))
        ]
        with jax.named_scope("to_section"):
            arrived.append(lax.ppermute(chunks[step], ("pipe", "expert"), pairs))
    arrived = [arrived[i] for i in (3, 1, 0, 2)]
    return jnp.concatenate(arrived, axis=0)


def per_device(
    forward_input,
    forward_route,
    forward_weight,
    backward_input,
    backward_route,
    backward_weight,
    output_grad,
    norm_gain,
    gate_weight,
    up_weight,
    down_weight,
):
    tokens = forward_input.shape[1]
    capacity = max(2, 3 * tokens // (2 * EXPERTS))
    count = EXPERTS * capacity
    gain = norm_gain[0]
    own = (gate_weight[0], up_weight[0], down_weight[0])

    def onehot(target):
        return (jnp.arange(count)[:, None] == target[None, :]).astype(BF)

    ahead_table, ahead_first, _ = (onehot(target) for target in slots_of(forward_route[0], capacity))
    behind_table, _, _ = (onehot(target) for target in slots_of(backward_route[0], capacity))
    sections = lax.axis_size("pipe")
    ahead = [(i, (i + 1) % sections) for i in range(sections)]
    size = count // PAIRS
    ahead_kinds = on_core(pick_body, size, PAIRS, forward_input[0], norm_gain, ahead_first)
    behind_wide, behind_scale = normalize(backward_input[0])
    behind_normed = (behind_wide * behind_scale * gain).astype(BF)
    routed_grad = (output_grad[0].astype(F32) * backward_weight[0]).astype(BF)
    to_x, to_class = swap_order(PAIRS, XS, capacity), swap_order(XS, PAIRS, capacity)
    gate_other = moved(own[0], Y_SWAP, "gate_swap")
    up_other = moved(after(gate_other, own[1]), Y_SWAP, "up_swap")
    down_other = moved(after(up_other, own[2]), Y_SWAP, "down_swap")
    weights = own + (gate_other, up_other, down_other)

    behind_slots, grad_slots = pick(behind_table, behind_normed), pick(behind_table, routed_grad)
    behind_kinds = on_core(sort_body, size, PAIRS, along_x(behind_slots), to_class)
    grad_kinds = on_core(sort_body, size, PAIRS, along_x(grad_slots), to_class)
    ahead_held = outward(ahead_kinds, (gain,) * 3, "ahead_outward")
    (near, far), ahead_rows = paired(ahead_held, COSTS[:2], gain, "ahead_pair")
    behind_held = outward(behind_kinds, (near, far, far), "behind_outward")
    behind_held[1] = after(gate_other, behind_held[1])
    behind_held[3] = after(up_other, behind_held[3])
    (near, far), behind_rows = paired(behind_held, COSTS[2:4], ahead_rows[1], "behind_pair")
    grad_held = outward(grad_kinds, (near, far, far), "grad_outward")
    grad_held[3] = after(down_other, grad_held[3])
    _, grad_rows = paired(grad_held, COSTS[4:], behind_rows[1], "grad_pair")

    ahead_both = along_x(on_core(spread_body, 2 * count, 1, *ahead_held, *ahead_rows, to_x)[0])
    ahead_parts = on_core(forward_body, count // 2, 4, ahead_both, to_class, *weights)
    behind_parts = on_core(
        backward_body, count // 2, 4, *behind_held, *behind_rows, *grad_held, *grad_rows[:1],
        after(ahead_parts, grad_rows[1]), *weights
    )
    ahead_home, others = returned(ahead_parts[:2], ahead_parts[2:], gain, "ahead_return")
    behind_home, _ = returned(behind_parts[:2], behind_parts[2:], others, "behind_return")
    ahead_back = along_x(pick(to_x, ahead_home))

    with jax.named_scope("behind_late"):
        late_rows = jnp.concatenate([backward_input[0], output_grad[0]], axis=0)
        late_rows = lax.ppermute(after(down_other, late_rows), "pipe", backwards(ahead))
        late_small = jnp.zeros((2, gain.shape[0]), F32).at[0].set(gain)
        late_small = late_small.at[1, :tokens].set(backward_route[0, :, 0].astype(F32))
        late_small = lax.ppermute(after(down_other, late_small), "pipe", backwards(ahead))
    collect = (((0,), (0,)), ((), ()))
    mixed = lax.dot_general(ahead_table, ahead_back, collect, preferred_element_type=F32)
    section_out = (forward_input[0].astype(F32) + mixed * forward_weight[0]).astype(BF)
    next_input = lax.ppermute(section_out, "pipe", ahead)
    behind_back = to_section(after(next_input, behind_home), capacity, -1)
    late_gain, late_route = late_small[0], late_small[1, :tokens].astype(jnp.int32)
    late_table = onehot(slots_of(late_route, capacity)[2])
    normed_grad = lax.dot_general(late_table, behind_back, collect, preferred_element_type=F32)
    late_wide, late_scale = normalize(late_rows[:tokens])
    unit = late_wide * late_scale
    unit_grad = late_gain * normed_grad
    previous_grad = late_rows[tokens:].astype(F32) + late_scale * (
        unit_grad - unit * jnp.mean(unit_grad * unit, axis=-1, keepdims=True)
    )
    return (next_input[None], previous_grad.astype(BF)[None])


def solution(mesh):
    rows = P("pipe", "expert", None)
    columns = P("pipe", None, "expert")
    return jax.shard_map(
        per_device,
        mesh=mesh,
        in_specs=(rows,) * 7 + (P("pipe", None), columns, columns, rows),
        out_specs=(rows, rows),
        check_vma=False,
    )
```

```python
import jax
import jax.numpy as jnp
from jax import lax
from jax.experimental import pallas as pl
from jax.experimental.pallas import tpu as pltpu
from jax.sharding import PartitionSpec as P

EPS = 1e-06
XS, ZS, YS = 4, 8, 2
PAIRS = 4
EXPERTS = 16
BF = jnp.bfloat16
F32 = jnp.float32
COSTS = (20_000_000_000, 15_000_000_000, 5_000_000_000, 40_000_000_000, 5_000_000_000, 40_000_000_000)


def place(x, z, y):
    return (x % XS) * (ZS * YS) + (z % ZS) * YS + y


def hop(move):
    return [
        (place(x, z, y), place(*move(x, z, y)))
        for x in range(XS)
        for z in range(ZS)
        for y in range(YS)
    ]


def backwards(pairs):
    return [(b, a) for a, b in pairs]


Y_SWAP = hop(lambda x, z, y: (x, z, 1 - y))
Z_SWAP = hop(lambda x, z, y: (x, z ^ 1, y))
NEAR = hop(lambda x, z, y: (x, z - 1 if z % 2 == 0 else z + 1, y))
MIDDLE = hop(lambda x, z, y: (x, z + 2 if z % 2 == 0 else z - 2, y))
FAR = hop(lambda x, z, y: (x, z - 3 if z % 2 == 0 else z + 3, y))
OUTWARD = (NEAR, MIDDLE, FAR)
HOMEWARD = tuple(backwards(pairs) for pairs in OUTWARD)
X_GROUPS = [[place(x, z, y) for x in range(XS)] for z in range(ZS) for y in range(YS)]


def moved(array, pairs, name=None):
    if name is None:
        return lax.ppermute(array, "expert", pairs)
    with jax.named_scope(name):
        return lax.ppermute(array, "expert", pairs)


def along_x(rows):
    count, width = rows.shape
    chunks = rows.reshape(XS, count // XS, width)
    chunks = lax.all_to_all(
        chunks, "expert", split_axis=0, concat_axis=0, tiled=True, axis_index_groups=X_GROUPS
    )
    return chunks.reshape(count, width)


def normalize(values):
    widened = values.astype(F32)
    scale = lax.rsqrt(jnp.mean(widened * widened, axis=-1, keepdims=True) + EPS)
    return (widened, scale)


def slots_of(routes, capacity):
    flat = routes.reshape(-1)
    tokens = flat.shape[0]
    here = lax.axis_index("expert")
    z = (here // YS) % ZS
    pair, parity = z // 2, z % 2
    steps = (flat % PAIRS - pair) % PAIRS
    kind = jnp.where(
        steps == 0, 0, jnp.where(steps == 2, 3, jnp.where((steps == 1) == (parity == 1), 1, 2))
    )
    earlier = jnp.arange(tokens)[None, :] < jnp.arange(tokens)[:, None]
    rank = jnp.sum(((flat[:, None] == flat[None, :]) & earlier).astype(jnp.int32), axis=1)
    x = flat // PAIRS
    steps = (here // (ZS * YS) - x) % XS
    return tuple(
        place * capacity + rank for place in (x * PAIRS + kind, kind * XS + x, steps * PAIRS + kind)
    )


def swap_order(outer, inner, block):
    count = outer * inner * block
    row = jnp.arange(count)
    i, o, r = row // (outer * block), (row // block) % outer, row % block
    source = (o * inner + i) * block + r
    return (source[:, None] == jnp.arange(count)[None, :]).astype(BF)


def pick(onehot, rows):
    return jnp.dot(onehot, rows, preferred_element_type=F32).astype(BF)


def after(done, later):
    return lax.optimization_barrier((done, later))[1]


def split(rows):
    size = rows.shape[0] // PAIRS
    return [rows[i * size : (i + 1) * size] for i in range(PAIRS)]


def outward(kinds, earlier, name):
    sent = [
        moved(after(done, kind), pairs, name)
        for done, kind, pairs in zip(earlier, kinds[1:], OUTWARD)
    ]
    return [kinds[0]] + sent


def paired(kinds, costs, before, name):
    size = kinds[0].shape[0]
    groups = [
        on_core(stack_body, 2 * size, 1, *kinds[2 * i : 2 * i + 2], cost=costs[i])[0]
        for i in range(2)
    ]
    near = moved(after(before, groups[0]), Z_SWAP, name)
    return groups, (near, moved(after(near, groups[1]), Z_SWAP, name))


def returned(mine, partner, before, name):
    size = mine[0].shape[0] // 2
    far_other = moved(after(before, partner[1]), Z_SWAP, name)
    near_other = moved(after(before, partner[0]), Z_SWAP, name)
    far = added(mine[1], far_other)
    near = added(mine[0], near_other)
    back = [
        near[:size],
        moved(near[size:], HOMEWARD[0], name),
        moved(far[:size], HOMEWARD[1], name),
        moved(far[size:], HOMEWARD[2], name),
    ]
    return jnp.concatenate(back, axis=0), (far_other, near_other)


def added(mine, other):
    return (mine.astype(F32) + other.astype(F32)).astype(BF)


def mm(a, b):
    return jnp.dot(a, b, preferred_element_type=F32)


def mm_t(a, b):
    return lax.dot_general(a, b, (((1,), (1,)), ((), ())), preferred_element_type=F32)


def joined(refs):
    return jnp.concatenate([ref[...] for ref in refs], axis=0)


def pick_body(values, gain, table, *outs):
    widened = values[...].astype(F32)
    scale = lax.rsqrt(jnp.mean(widened * widened, axis=-1, keepdims=True) + EPS)
    picked = mm(table[...], (widened * scale * gain[...]).astype(BF)).astype(BF)
    cut(picked, outs)


def cut(rows, outs):
    size = outs[0].shape[0]
    for i, out in enumerate(outs):
        out[...] = rows[i * size : (i + 1) * size]


def sort_body(arrived, order, *outs):
    cut(mm(order[...], arrived[...]).astype(BF), outs)


def stack_body(*refs):
    size = refs[0].shape[0]
    for i, ref in enumerate(refs[:-1]):
        refs[-1][i * size : (i + 1) * size, :] = ref[...]


def spread_body(own, near, middle, far, partner_a, partner_b, order, out):
    size = out.shape[0] // (2 * XS)
    for half, refs in enumerate(((own, near, middle, far), (partner_a, partner_b))):
        picked = mm(order[...], joined(refs)).astype(BF)
        for x in range(XS):
            start = (2 * x + half) * size
            out[start : start + size, :] = picked[x * size : (x + 1) * size]


def halves(rows, order):
    size = rows.shape[0] // (2 * XS)
    picked = []
    for half in range(2):
        chosen = [rows[(2 * x + half) * size : (2 * x + half + 1) * size] for x in range(XS)]
        picked.append(mm(order[...], jnp.concatenate(chosen, axis=0)).astype(BF))
    return picked


def forward_body(rows, order, gate_a, up_a, down_a, gate_b, up_b, down_b, *outs):
    x = rows[...]
    total = None
    for gate_cols, up_cols, down_rows in ((gate_a, up_a, down_a), (gate_b, up_b, down_b)):
        gate_pre = mm(x, gate_cols[...])
        up_pre = mm(x, up_cols[...])
        hidden = (gate_pre / (1.0 + jnp.exp(-gate_pre)) * up_pre).astype(BF)
        part = mm(hidden, down_rows[...])
        total = part if total is None else total + part
    for half, picked in enumerate(halves(total.astype(BF), order)):
        cut(picked, outs[2 * half : 2 * half + 2])


def backward_body(*refs):
    gate_a, up_a, down_a, gate_b, up_b, down_b = refs[12:18]
    x, g = joined(refs[:6]), joined(refs[6:12])
    total = None
    for gate_cols, up_cols, down_rows in ((gate_a, up_a, down_a), (gate_b, up_b, down_b)):
        gate_back = mm(x, gate_cols[...])
        up_back = mm(x, up_cols[...])
        hidden_grad = mm_t(g, down_rows[...])
        sigmoid_gate = 1.0 / (1.0 + jnp.exp(-gate_back))
        gate_grad = (
            hidden_grad * up_back * sigmoid_gate * (1.0 + gate_back * (1.0 - sigmoid_gate))
        ).astype(BF)
        up_grad = (hidden_grad * gate_back * sigmoid_gate).astype(BF)
        part = mm_t(gate_grad, gate_cols[...]) + mm_t(up_grad, up_cols[...])
        total = part if total is None else total + part
    cut(total.astype(BF), refs[18:])


def on_core(body, rows, outs, *operands, cost=0):
    shape = jax.ShapeDtypeStruct((rows, operands[0].shape[1]), BF)
    whole = pl.BlockSpec(memory_space=pltpu.VMEM)
    return pl.pallas_call(
        body,
        out_shape=(shape,) * outs,
        in_specs=[whole] * len(operands),
        out_specs=(whole,) * outs,
        compiler_params=pltpu.CompilerParams(vmem_limit_bytes=56 * 1024 * 1024),
        cost_estimate=pl.CostEstimate(flops=cost, bytes_accessed=0, transcendentals=0),
    )(*operands)


def to_section(rows, block, shift):
    count = rows.shape[0]
    here = lax.axis_index("expert") // (ZS * YS)
    row = jnp.arange(count)
    step, kind, rank = row // (PAIRS * block), (row // block) % PAIRS, row % block
    source = (kind * XS + (here + step) % XS) * block + rank
    chunks = split(pick((source[:, None] == row[None, :]).astype(BF), rows))
    sections, devices = lax.axis_size("pipe"), XS * ZS * YS
    arrived = []
    for step in (2, 1, 3, 0):
        pairs = [
            (s * devices + a, (s + shift) % sections * devices + b)
            for s in range(sections)
            for a, b in hop(lambda x, z, y: (x + step, z, y))
        ]
        with jax.named_scope("to_section"):
            arrived.append(lax.ppermute(chunks[step], ("pipe", "expert"), pairs))
    arrived = [arrived[i] for i in (3, 1, 0, 2)]
    return jnp.concatenate(arrived, axis=0)


def per_device(
    forward_input,
    forward_route,
    forward_weight,
    backward_input,
    backward_route,
    backward_weight,
    output_grad,
    norm_gain,
    gate_weight,
    up_weight,
    down_weight,
):
    tokens = forward_input.shape[1]
    capacity = max(2, 3 * tokens // (2 * EXPERTS))
    count = EXPERTS * capacity
    gain = norm_gain[0]
    own = (gate_weight[0], up_weight[0], down_weight[0])

    def onehot(target):
        return (jnp.arange(count)[:, None] == target[None, :]).astype(BF)

    ahead_table, ahead_first, _ = (onehot(target) for target in slots_of(forward_route[0], capacity))
    sections = lax.axis_size("pipe")
    ahead = [(i, (i + 1) % sections) for i in range(sections)]
    size = count // PAIRS
    ahead_kinds = on_core(pick_body, size, PAIRS, forward_input[0], norm_gain, ahead_first)
    later_route, gain = after(ahead_kinds[0], (backward_route[0], gain))
    behind_table, _, _ = (onehot(target) for target in slots_of(later_route, capacity))
    behind_wide, behind_scale = normalize(backward_input[0])
    behind_normed = (behind_wide * behind_scale * gain).astype(BF)
    routed_grad = (output_grad[0].astype(F32) * backward_weight[0]).astype(BF)
    to_x, to_class = swap_order(PAIRS, XS, capacity), swap_order(XS, PAIRS, capacity)
    gate_other = moved(own[0], Y_SWAP, "gate_swap")
    up_other = moved(after(gate_other, own[1]), Y_SWAP, "up_swap")
    down_other = moved(after(up_other, own[2]), Y_SWAP, "down_swap")
    weights = own + (gate_other, up_other, down_other)

    behind_slots, grad_slots = pick(behind_table, behind_normed), pick(behind_table, routed_grad)
    behind_kinds = on_core(sort_body, size, PAIRS, along_x(behind_slots), to_class)
    grad_kinds = on_core(sort_body, size, PAIRS, along_x(grad_slots), to_class)
    ahead_held = outward(ahead_kinds, (ahead_kinds[0],) * 3, "ahead_outward")
    (near, far), ahead_rows = paired(ahead_held, COSTS[:2], ahead_kinds[0], "ahead_pair")
    behind_held = outward(behind_kinds, (near, far, far), "behind_outward")
    behind_held[1] = after(gate_other, behind_held[1])
    behind_held[3] = after(up_other, behind_held[3])
    (near, far), behind_rows = paired(behind_held, COSTS[2:4], ahead_rows[1], "behind_pair")
    grad_held = outward(grad_kinds, (near, far, far), "grad_outward")
    grad_held[3] = after(down_other, grad_held[3])
    _, grad_rows = paired(grad_held, COSTS[4:], behind_rows[1], "grad_pair")

    ahead_both = along_x(on_core(spread_body, 2 * count, 1, *ahead_held, *ahead_rows, to_x)[0])
    ahead_parts = on_core(forward_body, count // 2, 4, ahead_both, to_class, *weights)
    behind_parts = on_core(
        backward_body, count // 2, 4, *behind_held, *behind_rows, *grad_held, *grad_rows[:1],
        after(ahead_parts, grad_rows[1]), *weights
    )
    ahead_home, others = returned(ahead_parts[:2], ahead_parts[2:], gain, "ahead_return")
    behind_home, _ = returned(behind_parts[:2], behind_parts[2:], others, "behind_return")
    ahead_back = along_x(pick(to_x, ahead_home))

    with jax.named_scope("behind_late"):
        late_rows = jnp.concatenate([backward_input[0], output_grad[0]], axis=0)
        late_rows = lax.ppermute(after(down_other, late_rows), "pipe", backwards(ahead))
        late_small = jnp.zeros((2, gain.shape[0]), F32).at[0].set(gain)
        late_small = late_small.at[1, :tokens].set(backward_route[0, :, 0].astype(F32))
        late_small = lax.ppermute(after(down_other, late_small), "pipe", backwards(ahead))
    collect = (((0,), (0,)), ((), ()))
    mixed = lax.dot_general(ahead_table, ahead_back, collect, preferred_element_type=F32)
    section_out = (forward_input[0].astype(F32) + mixed * forward_weight[0]).astype(BF)
    next_input = lax.ppermute(section_out, "pipe", ahead)
    behind_back = to_section(after(next_input, behind_home), capacity, -1)
    late_gain, late_route = late_small[0], late_small[1, :tokens].astype(jnp.int32)
    late_table = onehot(slots_of(late_route, capacity)[2])
    normed_grad = lax.dot_general(late_table, behind_back, collect, preferred_element_type=F32)
    late_wide, late_scale = normalize(late_rows[:tokens])
    unit = late_wide * late_scale
    unit_grad = late_gain * normed_grad
    previous_grad = late_rows[tokens:].astype(F32) + late_scale * (
        unit_grad - unit * jnp.mean(unit_grad * unit, axis=-1, keepdims=True)
    )
    return (next_input[None], previous_grad.astype(BF)[None])


def solution(mesh):
    rows = P("pipe", "expert", None)
    columns = P("pipe", None, "expert")
    return jax.shard_map(
        per_device,
        mesh=mesh,
        in_specs=(rows,) * 7 + (P("pipe", None), columns, columns, rows),
        out_specs=(rows, rows),
        check_vma=False,
    )
```
